32 devices in a mesh: group: 2 (over x), fiber: 16 (over z, y, core).
Axes of the slice: x: 2, y: 2, z: 4, core: 2. Of those that a mesh axis runs over, the one named last changes fastest.
Arguments:
- traces: bfloat16 [1536, 50176], P(('group', 'fiber')), parts along dimension 0, may hold values from -32 to 32
- live_mask: int32 [1536], P(('group', 'fiber')), parts along dimension 0, may hold values from 0 to 1
- source_channels: int32 [4, 8], P('group'), parts along dimension 0, may hold values from 0 to 47
- source_owner: int32 [4], P('group'), parts along dimension 0, may hold values from 0 to 15
Outputs:
- cross_spectra: float32 [2, 8, 1536, 2048], P(None, None, ('group', 'fiber')), parts along dimension 2
The draws below stay inside these ranges and needn't reach their ends.
There are 2 independent parts, one for each index of `group`. The reference program is written for one: setup_inputs(seed, part) draws one part's arguments, and reference() takes and returns one part's arrays. A program takes and returns all parts, laid end to end along the dimension named above; each array names one. Nothing has to cross between parts.
All inputs are finite; a program needn't handle non-finite values.
Results may differ from the reference program's by a relative error of at most 0.00073.
Values may be sent and summed in bfloat16 or wider, within the bound.
A program may use at most 128 MiB of HBM per device.

```python
import jax
import jax.numpy as jnp
from jax import lax

FRAME = 2048
SMOOTH = 64
RIM = 8
CH_DEV = 48
STEPS = 2
NSRC = 8
SAMPLES = 50176
CHANNELS = 768
N_FIBER = 16


def draw_traces(key, part):
    subkeys = jax.random.split(jax.random.fold_in(key, 11), 6)
    noise_part = jax.random.normal(subkeys[0], (CHANNELS, SAMPLES), jnp.float32)
    channel_scale = jnp.exp(jax.random.uniform(subkeys[2], (CHANNELS,), jnp.float32, jnp.log(0.5), jnp.log(3.0)))
    frequency = jax.random.uniform(subkeys[3], (6,), jnp.float32, 0.02, 0.48)
    sample_time = jnp.arange(SAMPLES, dtype=jnp.float32)
    phase_angle = 2.0 * jnp.pi * jnp.mod(frequency[:, None] * sample_time[None, :], 1.0)
    amplitude = jnp.exp(jax.random.uniform(subkeys[4], (CHANNELS, 6), jnp.float32, jnp.log(0.2), jnp.log(1.2)))
    line_shift = jax.random.uniform(subkeys[5], (CHANNELS, 6), jnp.float32, -jnp.pi, jnp.pi)
    line_part = jnp.dot(amplitude * jnp.cos(line_shift), jnp.sin(phase_angle), precision=lax.Precision.HIGHEST)
    line_part = line_part + jnp.dot(amplitude * jnp.sin(line_shift), jnp.cos(phase_angle), precision=lax.Precision.HIGHEST)
    values = channel_scale[:, None] * (noise_part + line_part)
    return jnp.clip(values, -32.0, 32.0).astype(jnp.bfloat16)


def draw_live_mask(key, part):
    subkeys = jax.random.split(jax.random.fold_in(key, 23), 3)
    isolated = jax.random.randint(subkeys[0], (CHANNELS,), 0, 16) == 0
    run_start = jax.random.randint(subkeys[1], (), 0, CHANNELS - 2 * CH_DEV + 1)
    length = jax.random.randint(subkeys[2], (), CH_DEV // 2, 2 * CH_DEV + 1)
    position = jnp.arange(CHANNELS, dtype=jnp.int32)
    in_run = (position >= run_start) & (position < run_start + length)
    return jnp.where(isolated | in_run, 0, 1).astype(jnp.int32)


def with_ends(entries, key, smallest, high):
    shape = entries.shape
    index_at = [jax.random.randint(jax.random.fold_in(key, axis), (), 0, shape[axis]) for axis in range(len(shape))]
    entries = entries.at[tuple(index_at)].set(smallest)
    longest = shape.index(max(shape))
    index_at[longest] = (index_at[longest] + 1) % shape[longest]
    return entries.at[tuple(index_at)].set(high)


def setup_inputs(seed: int = 0, part: int = 0) -> dict:
    splits = jax.random.split(jax.random.key(seed), 5)
    part_keys = jax.random.split(jax.random.fold_in(splits[4], part), 5)
    traces = draw_traces(jax.random.fold_in(jax.random.fold_in(splits[4], part), 71), part)
    live_mask = draw_live_mask(jax.random.fold_in(jax.random.fold_in(splits[4], part), 71), part)
    source_channels = with_ends(jax.random.randint(part_keys[2], (STEPS, NSRC), 0, CH_DEV), jax.random.fold_in(part_keys[2], 1), 0, CH_DEV - 1).astype(jnp.int32)
    source_owner = jax.random.randint(part_keys[3], (STEPS,), 0, N_FIBER).astype(jnp.int32)
    return dict(traces=traces, live_mask=live_mask, source_channels=source_channels, source_owner=source_owner)


def dft_table(frame_len):
    sample_pos = jnp.arange(frame_len, dtype=jnp.int32)
    bin_pos = jnp.arange(frame_len // 2, dtype=jnp.int32)
    product = sample_pos[:, None] * bin_pos[None, :] % frame_len
    phase_angle = 2.0 * jnp.pi / frame_len * product.astype(jnp.float32)
    hann_window = 0.5 - 0.5 * jnp.cos(2.0 * jnp.pi / frame_len * sample_pos.astype(jnp.float32))
    cosine = hann_window[:, None] * jnp.cos(phase_angle)
    sine = -hann_window[:, None] * jnp.sin(phase_angle)
    return jnp.concatenate([cosine, sine], axis=1).astype(jnp.bfloat16)

def band_matrix(num_bins, half_width):
    bin_pos = jnp.arange(num_bins, dtype=jnp.int32)
    inside = jnp.abs(bin_pos[:, None] - bin_pos[None, :]) <= half_width
    band = inside.astype(jnp.bfloat16)
    bin_count = lax.optimization_barrier(jnp.sum(inside.astype(jnp.float32), axis=0))
    return (band, bin_count)

def spatial_filter(padded, live, rim_width):
    channels = padded.shape[0] - 2 * rim_width
    center = padded[rim_width:rim_width + channels].astype(jnp.float32)
    neighbour_sum = jnp.zeros(center.shape, jnp.float32)
    for offset in range(1, rim_width + 1):
        weight = (rim_width + 1 - offset) / (rim_width * (rim_width + 1.0))
        lower = padded[rim_width - offset:rim_width - offset + channels].astype(jnp.float32)
        upper = padded[rim_width + offset:rim_width + offset + channels].astype(jnp.float32)
        neighbour_sum = neighbour_sum + weight * (lower + upper)
    return (live[:, None] * (center - neighbour_sum)).astype(jnp.bfloat16)

def whiten_rows(filtered, frame_len, half_width):
    rows, samples = filtered.shape
    hop_len = frame_len // 2
    num_frames = samples // hop_len - 1
    num_bins = frame_len // 2
    blocks = filtered.reshape(rows, num_frames + 1, hop_len)
    frames = jnp.concatenate([blocks[:, :-1], blocks[:, 1:]], axis=2).reshape(rows * num_frames, frame_len)
    spectra = jnp.dot(frames, dft_table(frame_len), preferred_element_type=jnp.float32)
    real_part = spectra[:, :num_bins]
    imag_part = spectra[:, num_bins:]
    spectral_power = (real_part * real_part + imag_part * imag_part).astype(jnp.bfloat16)
    band, bin_count = band_matrix(num_bins, half_width)
    smooth = jnp.dot(spectral_power, band, preferred_element_type=jnp.float32) / bin_count[None, :]
    factor = lax.rsqrt(smooth + 1e-06)
    whitened = jnp.concatenate([real_part * factor, imag_part * factor], axis=1).astype(jnp.bfloat16)
    return whitened.reshape(rows, num_frames, frame_len)

def reference(traces, live_mask, source_channels, source_owner):
    channels = traces.shape[0]
    num_bins = FRAME // 2
    premasked = traces * live_mask.astype(jnp.bfloat16)[:, None]
    padded = jnp.concatenate([jnp.zeros((RIM, traces.shape[1]), jnp.bfloat16), premasked, jnp.zeros((RIM, traces.shape[1]), jnp.bfloat16)], axis=0)
    filtered = spatial_filter(padded, live_mask.astype(jnp.float32), RIM)
    whitened = whiten_rows(filtered, FRAME, SMOOTH)
    global_rows = (source_owner[:, None] * CH_DEV + source_channels).astype(jnp.int32)
    sources = whitened[global_rows].astype(jnp.float32)
    whole = whitened.astype(jnp.float32)
    num_frames = whitened.shape[1]
    src_real = sources[..., :num_bins]
    src_imag = sources[..., num_bins:]
    dst_real = whole[..., :num_bins]
    dst_imag = whole[..., num_bins:]
    real_out = jnp.einsum('snfk,cfk->snck', src_real, dst_real) + jnp.einsum('snfk,cfk->snck', src_imag, dst_imag)
    imag_out = jnp.einsum('snfk,cfk->snck', src_real, dst_imag) - jnp.einsum('snfk,cfk->snck', src_imag, dst_real)
    return jnp.concatenate([real_out, imag_out], axis=3) / num_frames
```

```python
import functools

import jax
import jax.numpy as jnp
import numpy as np
from jax import lax
from jax.experimental import pallas as pl
from jax.experimental.pallas import tpu as pltpu
from jax.sharding import PartitionSpec as P

FRAME = 2048
HOP = FRAME // 2
BINS = FRAME // 2
SMOOTH = 64
RIM = 8
LANES = 128
VMEM = 56 * 1024 * 1024


def dft_table():
    n = np.arange(FRAME)
    k = np.arange(BINS)
    phase = 2.0 * np.pi / FRAME * (n[:, None] * k[None, :] % FRAME)
    hann = 0.5 - 0.5 * np.cos(2.0 * np.pi / FRAME * n)
    table = np.concatenate(
        [hann[:, None] * np.cos(phase), -hann[:, None] * np.sin(phase)], axis=1
    )
    return table.astype(np.float32).astype(jnp.bfloat16)


def band_matrix():
    k = np.arange(BINS)
    inside = np.abs(k[:, None] - k[None, :]) <= SMOOTH
    recip = (1.0 / inside.sum(axis=0)).astype(np.float32)
    return inside.astype(np.float32).astype(jnp.bfloat16), recip[None, :]


def tap_matrix(channels):
    place = np.concatenate(
        [np.arange(channels), np.arange(-RIM, 0), np.arange(channels, channels + RIM)]
    )
    distance = np.abs(np.arange(channels)[:, None] - place[None, :])
    taps = np.where(distance <= RIM, -(RIM + 1.0 - distance), 0.0)
    return np.where(distance == 0, RIM * (RIM + 1.0), taps).astype(np.float32)


def filter_kernel(channels, weight_ref, own_ref, low_ref, high_ref, out_ref, src_ref):
    rows = jnp.concatenate([own_ref[...], low_ref[...], high_ref[...]], axis=0)
    total = jnp.dot(weight_ref[...], rows, preferred_element_type=jnp.float32)
    total = (total * (1.0 / (RIM * (RIM + 1.0)))).astype(jnp.bfloat16)
    out_ref[...] = total[:channels]
    src_ref[...] = total[channels:]


def spatial_filter(weight, own, low, high):
    channels, samples = own.shape
    sources = weight.shape[0] - channels
    blocks = samples // HOP
    chunk = HOP * (7 if blocks % 7 == 0 else 1)
    columns = lambda rows: pl.BlockSpec((rows, chunk), lambda i: (0, i))
    return pl.pallas_call(
        functools.partial(filter_kernel, channels),
        grid=(samples // chunk,),
        in_specs=[
            pl.BlockSpec(weight.shape, lambda i: (0, 0)),
            columns(channels),
            columns(RIM),
            columns(RIM),
        ],
        out_specs=[columns(channels), columns(sources)],
        out_shape=[
            jax.ShapeDtypeStruct((channels, samples), jnp.bfloat16),
            jax.ShapeDtypeStruct((sources, samples), jnp.bfloat16),
        ],
        compiler_params=pltpu.CompilerParams(vmem_limit_bytes=VMEM),
        name="spatial_filter",
    )(weight, own, low, high)


def whiten_kernel(count, x_ref, table_ref, band_ref, recip_ref, out_ref, spec_ref, pow_ref):
    rows = x_ref.shape[0]
    first = pl.program_id(0) * count
    frames = jnp.concatenate(
        [
            x_ref[:, pl.ds(pl.multiple_of((first + i) * HOP, HOP), FRAME)]
            for i in range(count)
        ],
        axis=0,
    )
    width = 256
    for lo in range(0, BINS, width):
        real = jnp.dot(
            frames, table_ref[:, lo : lo + width], preferred_element_type=jnp.float32
        )
        imag = jnp.dot(
            frames,
            table_ref[:, BINS + lo : BINS + lo + width],
            preferred_element_type=jnp.float32,
        )
        spec_ref[:, lo : lo + width] = real
        spec_ref[:, BINS + lo : BINS + lo + width] = imag
        pow_ref[:, lo : lo + width] = (real * real + imag * imag).astype(jnp.bfloat16)
    for lo in range(0, BINS, width):
        start, stop = max(0, lo - LANES), min(BINS, lo + width + LANES)
        smooth = jnp.dot(
            pow_ref[:, start:stop],
            band_ref[start:stop, lo : lo + width],
            preferred_element_type=jnp.float32,
        )
        factor = lax.rsqrt(smooth * recip_ref[:, lo : lo + width] + 1e-06)
        for at in (lo, BINS + lo):
            white = (spec_ref[:, at : at + width] * factor).astype(jnp.bfloat16)
            for i in range(count):
                out_ref[i, :, at : at + width] = white[i * rows : (i + 1) * rows]


def whiten(filtered, count):
    rows, samples = filtered.shape
    frames = samples // HOP - 1
    band, recip = band_matrix()
    whole = lambda shape: pl.BlockSpec(
        shape, lambda i: (0,) * len(shape), pipeline_mode=pl.Buffered(1)
    )
    return pl.pallas_call(
        functools.partial(whiten_kernel, count),
        grid=(frames // count,),
        in_specs=[
            whole((rows, samples)),
            whole((FRAME, FRAME)),
            whole((BINS, BINS)),
            whole((1, BINS)),
        ],
        out_specs=pl.BlockSpec((count, rows, FRAME), lambda i: (i, 0, 0)),
        out_shape=jax.ShapeDtypeStruct((frames, rows, FRAME), jnp.bfloat16),
        scratch_shapes=[
            pltpu.VMEM((count * rows, FRAME), jnp.float32),
            pltpu.VMEM((count * rows, BINS), jnp.bfloat16),
        ],
        compiler_params=pltpu.CompilerParams(vmem_limit_bytes=VMEM),
        cost_estimate=pl.CostEstimate(
            flops=2 * frames * rows * FRAME * FRAME,
            bytes_accessed=8 * FRAME * FRAME,
            transcendentals=frames * rows * BINS,
        ),
        name="whiten",
    )(filtered, dft_table(), band, recip)


def cross_kernel(sr_ref, si_ref, wr_ref, wi_ref, out_ref, c_ref, d_ref, e_ref, a_ref, p_ref, m_ref):
    frames, sources, _ = sr_ref.shape
    channels = wr_ref.shape[1]
    at = pl.multiple_of(pl.program_id(0) * LANES, LANES)

    @pl.loop(0, frames)
    def _(f):
        c = wr_ref[f].astype(jnp.float32)
        d = wi_ref[f].astype(jnp.float32)
        c_ref[f] = c
        d_ref[f] = d
        e_ref[f] = c + d
        a = sr_ref[f].astype(jnp.float32) * (1.0 / frames)
        b = si_ref[f].astype(jnp.float32) * (1.0 / frames)
        a_ref[f] = a
        p_ref[f] = a + b
        m_ref[f] = b - a

    pieces = channels // 8
    together = 2
    for s in range(0, sources, together):

        def step(f, sums):
            sums = list(sums)
            taps = []
            for t in range(together):
                row = pl.ds(s + t, 1)
                taps.append(
                    tuple(
                        jnp.broadcast_to(ref[f, row, :], (8, LANES))
                        for ref in (a_ref, p_ref, m_ref)
                    )
                )
            for v in range(pieces):
                part = slice(8 * v, 8 * v + 8)
                c, d, e = c_ref[f, part, :], d_ref[f, part, :], e_ref[f, part, :]
                for t in range(together):
                    a, p, m = taps[t]
                    base = 3 * (t * pieces + v)
                    sums[base] = sums[base] + a * e
                    sums[base + 1] = sums[base + 1] + p * c
                    sums[base + 2] = sums[base + 2] + m * d
            return tuple(sums)

        zero = jnp.zeros((8, LANES), jnp.float32)
        sums = lax.fori_loop(0, frames, step, (zero,) * (3 * together * pieces), unroll=4)
        for t in range(together):
            for v in range(pieces):
                base = 3 * (t * pieces + v)
                part = slice(8 * v, 8 * v + 8)
                out_ref[s + t, part, pl.ds(at, LANES)] = sums[base] + sums[base + 2]
                out_ref[s + t, part, pl.ds(BINS + at, LANES)] = sums[base] - sums[base + 1]


def cross(sources, whitened):
    frames, channels, _ = whitened.shape
    count = sources.shape[1]
    tiles = BINS // LANES
    real = lambda rows: pl.BlockSpec((frames, rows, LANES), lambda j: (0, 0, j))
    imag = lambda rows: pl.BlockSpec((frames, rows, LANES), lambda j: (0, 0, tiles + j))
    tile = lambda rows: pltpu.VMEM((frames, rows, LANES), jnp.float32)
    return pl.pallas_call(
        cross_kernel,
        grid=(tiles,),
        in_specs=[real(count), imag(count), real(channels), imag(channels)],
        out_specs=pl.BlockSpec(
            (count, channels, FRAME), lambda j: (0, 0, 0), pipeline_mode=pl.Buffered(1)
        ),
        out_shape=jax.ShapeDtypeStruct((count, channels, FRAME), jnp.float32),
        scratch_shapes=[tile(channels)] * 3 + [tile(count)] * 3,
        compiler_params=pltpu.CompilerParams(vmem_limit_bytes=VMEM),
        name="cross",
    )(sources, sources, whitened, whitened)


def neighbours(live, traces):
    count = lax.axis_size("fiber")
    up = [(i, i + 1) for i in range(count - 1)]
    down = [(i + 1, i) for i in range(count - 1)]
    mask = live.astype(jnp.bfloat16)[:, None]
    low = lax.ppermute(traces[-RIM:] * mask[-RIM:], "fiber", up)
    high = lax.ppermute(traces[:RIM] * mask[:RIM], "fiber", down)
    return low, high


def filter_weights(live, source_channels, source_owner):
    channels = live.shape[0]
    alive = live.astype(jnp.float32)
    column = jnp.concatenate([alive, jnp.ones((2 * RIM,), jnp.float32)])
    weight = tap_matrix(channels) * alive[:, None] * column[None, :]
    mine = (source_owner == lax.axis_index("fiber"))[:, None]
    chosen = jnp.where(mine, source_channels, -1).reshape(-1)
    pick = chosen[:, None] == jnp.arange(channels)[None, :]
    picked = jnp.sum(jnp.where(pick[:, :, None], weight[None], 0.0), axis=1)
    return jnp.concatenate([weight, picked], axis=0).astype(jnp.bfloat16)


def on_device(traces, live_mask, source_channels, source_owner):
    steps, per_step = source_channels.shape
    low, high = neighbours(live_mask, traces)
    weight = filter_weights(live_mask, source_channels, source_owner)
    filtered, mine = spatial_filter(weight, traces, low, high)
    arrived = lax.psum(mine, "fiber")
    whitened = whiten(filtered, 8)
    sources = whiten(arrived, 16)
    out = cross(sources, whitened)
    return out.reshape(steps, per_step, live_mask.shape[0], FRAME)


def solution(mesh):
    placed = (P(("group", "fiber"), None), P(("group", "fiber")), P("group", None), P("group"))
    return jax.shard_map(
        on_device,
        mesh=mesh,
        in_specs=placed,
        out_specs=P(None, None, ("group", "fiber"), None),
        check_vma=False,
    )
```

```python
import functools

import jax
import jax.numpy as jnp
import numpy as np
from jax import lax
from jax.experimental import pallas as pl
from jax.experimental.pallas import tpu as pltpu
from jax.sharding import PartitionSpec as P

FRAME = 2048
HOP = FRAME // 2
BINS = FRAME // 2
SMOOTH = 64
RIM = 8
LANES = 128
VMEM = 56 * 1024 * 1024


def dft_table():
    n = np.arange(FRAME)
    k = np.arange(BINS)
    phase = 2.0 * np.pi / FRAME * (n[:, None] * k[None, :] % FRAME)
    hann = 0.5 - 0.5 * np.cos(2.0 * np.pi / FRAME * n)
    table = np.concatenate(
        [hann[:, None] * np.cos(phase), -hann[:, None] * np.sin(phase)], axis=1
    )
    return table.astype(np.float32).astype(jnp.bfloat16)


def band_matrix():
    k = np.arange(BINS)
    inside = np.abs(k[:, None] - k[None, :]) <= SMOOTH
    recip = (1.0 / inside.sum(axis=0)).astype(np.float32)
    return inside.astype(np.float32).astype(jnp.bfloat16), recip[None, :]


def tap_matrix(channels):
    place = np.concatenate(
        [np.arange(channels), np.arange(-RIM, 0), np.arange(channels, channels + RIM)]
    )
    distance = np.abs(np.arange(channels)[:, None] - place[None, :])
    taps = np.where(distance <= RIM, -(RIM + 1.0 - distance), 0.0)
    return np.where(distance == 0, RIM * (RIM + 1.0), taps).astype(np.float32)


def filter_kernel(channels, weight_ref, own_ref, low_ref, high_ref, out_ref, src_ref):
    rows = jnp.concatenate([own_ref[...], low_ref[...], high_ref[...]], axis=0)
    total = jnp.dot(weight_ref[...], rows, preferred_element_type=jnp.float32)
    total = (total * (1.0 / (RIM * (RIM + 1.0)))).astype(jnp.bfloat16)
    out_ref[...] = total[:channels]
    src_ref[...] = total[channels:]


def spatial_filter(weight, own, low, high):
    channels, samples = own.shape
    sources = weight.shape[0] - channels
    blocks = samples // HOP
    chunk = HOP * (7 if blocks % 7 == 0 else 1)
    columns = lambda rows: pl.BlockSpec((rows, chunk), lambda i: (0, i))
    return pl.pallas_call(
        functools.partial(filter_kernel, channels),
        grid=(samples // chunk,),
        in_specs=[
            pl.BlockSpec(weight.shape, lambda i: (0, 0)),
            columns(channels),
            columns(RIM),
            columns(RIM),
        ],
        out_specs=[columns(channels), columns(sources)],
        out_shape=[
            jax.ShapeDtypeStruct((channels, samples), jnp.bfloat16),
            jax.ShapeDtypeStruct((sources, samples), jnp.bfloat16),
        ],
        compiler_params=pltpu.CompilerParams(vmem_limit_bytes=VMEM),
        name="spatial_filter",
    )(weight, own, low, high)


def whiten_kernel(count, x_ref, table_ref, band_ref, recip_ref, out_ref, spec_ref, pow_ref):
    rows = x_ref.shape[0]
    first = pl.program_id(0) * count
    frames = jnp.concatenate(
        [
            x_ref[:, pl.ds(pl.multiple_of((first + i) * HOP, HOP), FRAME)]
            for i in range(count)
        ],
        axis=0,
    )
    width = 256
    for lo in range(0, BINS, width):
        real = jnp.dot(
            frames, table_ref[:, lo : lo + width], preferred_element_type=jnp.float32
        )
        imag = jnp.dot(
            frames,
            table_ref[:, BINS + lo : BINS + lo + width],
            preferred_element_type=jnp.float32,
        )
        spec_ref[:, lo : lo + width] = real
        spec_ref[:, BINS + lo : BINS + lo + width] = imag
        pow_ref[:, lo : lo + width] = (real * real + imag * imag).astype(jnp.bfloat16)
    for lo in range(0, BINS, width):
        start, stop = max(0, lo - LANES), min(BINS, lo + width + LANES)
        smooth = jnp.dot(
            pow_ref[:, start:stop],
            band_ref[start:stop, lo : lo + width],
            preferred_element_type=jnp.float32,
        )
        factor = lax.rsqrt(smooth * recip_ref[:, lo : lo + width] + 1e-06)
        for at in (lo, BINS + lo):
            white = (spec_ref[:, at : at + width] * factor).astype(jnp.bfloat16)
            for i in range(count):
                out_ref[i, :, at : at + width] = white[i * rows : (i + 1) * rows]


def whiten(filtered, count):
    rows, samples = filtered.shape
    frames = samples // HOP - 1
    band, recip = band_matrix()
    whole = lambda shape: pl.BlockSpec(
        shape, lambda i: (0,) * len(shape), pipeline_mode=pl.Buffered(1)
    )
    return pl.pallas_call(
        functools.partial(whiten_kernel, count),
        grid=(frames // count,),
        in_specs=[
            whole((rows, samples)),
            whole((FRAME, FRAME)),
            whole((BINS, BINS)),
            whole((1, BINS)),
        ],
        out_specs=pl.BlockSpec((count, rows, FRAME), lambda i: (i, 0, 0)),
        out_shape=jax.ShapeDtypeStruct((frames, rows, FRAME), jnp.bfloat16),
        scratch_shapes=[
            pltpu.VMEM((count * rows, FRAME), jnp.float32),
            pltpu.VMEM((count * rows, BINS), jnp.bfloat16),
        ],
        compiler_params=pltpu.CompilerParams(vmem_limit_bytes=VMEM),
        cost_estimate=pl.CostEstimate(
            flops=2 * frames * rows * FRAME * FRAME,
            bytes_accessed=8 * FRAME * FRAME,
            transcendentals=frames * rows * BINS,
        ),
        name="whiten",
    )(filtered, dft_table(), band, recip)


def cross_kernel(sr_ref, si_ref, wr_ref, wi_ref, out_ref, c_ref, d_ref, e_ref, a_ref, p_ref, m_ref):
    frames, sources, _ = sr_ref.shape
    channels = wr_ref.shape[1]
    at = pl.multiple_of(pl.program_id(0) * LANES, LANES)

    @pl.loop(0, frames)
    def _(f):
        c = wr_ref[f].astype(jnp.float32)
        d = wi_ref[f].astype(jnp.float32)
        c_ref[f] = c
        d_ref[f] = d
        e_ref[f] = c + d
        a = sr_ref[f].astype(jnp.float32) * (1.0 / frames)
        b = si_ref[f].astype(jnp.float32) * (1.0 / frames)
        a_ref[f] = a
        p_ref[f] = a + b
        m_ref[f] = b - a

    pieces = channels // 8
    together = 2
    for s in range(0, sources, together):

        def step(f, sums):
            sums = list(sums)
            taps = []
            for t in range(together):
                row = pl.ds(s + t, 1)
                taps.append(
                    tuple(
                        jnp.broadcast_to(ref[f, row, :], (8, LANES))
                        for ref in (a_ref, p_ref, m_ref)
                    )
                )
            for v in range(pieces):
                part = slice(8 * v, 8 * v + 8)
                c, d, e = c_ref[f, part, :], d_ref[f, part, :], e_ref[f, part, :]
                for t in range(together):
                    a, p, m = taps[t]
                    base = 3 * (t * pieces + v)
                    sums[base] = sums[base] + a * e
                    sums[base + 1] = sums[base + 1] + p * c
                    sums[base + 2] = sums[base + 2] + m * d
            return tuple(sums)

        zero = jnp.zeros((8, LANES), jnp.float32)
        sums = lax.fori_loop(0, frames, step, (zero,) * (3 * together * pieces), unroll=4)
        for t in range(together):
            for v in range(pieces):
                base = 3 * (t * pieces + v)
                part = slice(8 * v, 8 * v + 8)
                out_ref[s + t, part, pl.ds(at, LANES)] = sums[base] + sums[base + 2]
                out_ref[s + t, part, pl.ds(BINS + at, LANES)] = sums[base] - sums[base + 1]


def cross(sources, whitened):
    frames, channels, _ = whitened.shape
    count = sources.shape[1]
    tiles = BINS // LANES
    real = lambda rows: pl.BlockSpec((frames, rows, LANES), lambda j: (0, 0, j))
    imag = lambda rows: pl.BlockSpec((frames, rows, LANES), lambda j: (0, 0, tiles + j))
    tile = lambda rows: pltpu.VMEM((frames, rows, LANES), jnp.float32)
    return pl.pallas_call(
        cross_kernel,
        grid=(tiles,),
        in_specs=[real(count), imag(count), real(channels), imag(channels)],
        out_specs=pl.BlockSpec(
            (count, channels, FRAME), lambda j: (0, 0, 0), pipeline_mode=pl.Buffered(1)
        ),
        out_shape=jax.ShapeDtypeStruct((count, channels, FRAME), jnp.float32),
        scratch_shapes=[tile(channels)] * 3 + [tile(count)] * 3,
        compiler_params=pltpu.CompilerParams(vmem_limit_bytes=VMEM),
        name="cross",
    )(sources, sources, whitened, whitened)


def share_stages(size):
    return [1 << i for i in range(size.bit_length() - 1)]


def share_kernel(size, x_ref, out_ref, held, landed, result, send_sem, recv_sem):
    me = lax.axis_index("fiber")
    stages = share_stages(size)
    samples = x_ref.shape[1]
    length = held.shape[2]
    sides = [lax.rem(me // bit, 2) for bit in stages]
    partners = [me + bit - 2 * bit * side for bit, side in zip(stages, sides)]

    barrier = pltpu.get_barrier_semaphore()
    for partner in partners:
        pl.semaphore_signal(
            barrier,
            inc=1,
            device_id={"fiber": partner},
            device_id_type=pl.DeviceIdType.MESH,
        )
    for j in range(size):
        stop = min(samples, (j + 1) * length)
        if stop < (j + 1) * length:
            held[j] = jnp.zeros(held.shape[1:], held.dtype)
        if stop > j * length:
            held[j, :, : stop - j * length] = x_ref[:, j * length : stop]
    pl.semaphore_wait(barrier, len(stages))

    first, count, at = 0, size, 0
    firsts = []
    for i, side in enumerate(sides):
        count //= 2
        firsts.append(first)
        kept = first + side * count
        sent = first + (1 - side) * count
        copy = pltpu.make_async_remote_copy(
            src_ref=held.at[pl.ds(sent, count)],
            dst_ref=landed.at[pl.ds(at, count)],
            send_sem=send_sem.at[i],
            recv_sem=recv_sem.at[i],
            device_id={"fiber": partners[i]},
            device_id_type=pl.DeviceIdType.MESH,
        )
        copy.start()
        copy.wait()
        for j in range(count):
            held[kept + j] = held[kept + j] + landed[at + j]
        at += count
        first = kept
    result[first] = held[first]
    for i in reversed(range(len(stages))):
        copy = pltpu.make_async_remote_copy(
            src_ref=result.at[pl.ds(first, count)],
            dst_ref=result.at[pl.ds(first, count)],
            send_sem=send_sem.at[len(stages) + i],
            recv_sem=recv_sem.at[len(stages) + i],
            device_id={"fiber": partners[i]},
            device_id_type=pl.DeviceIdType.MESH,
        )
        copy.start()
        copy.wait()
        first = firsts[i]
        count *= 2
    for j in range(size):
        stop = min(samples, (j + 1) * length)
        if stop > j * length:
            out_ref[:, j * length : stop] = result[j, :, : stop - j * length]


def share(mine):
    rows, samples = mine.shape
    size = lax.axis_size("fiber")
    length = -(-samples // (size * LANES)) * LANES
    stages = len(share_stages(size))
    blocks = lambda count: pltpu.VMEM((count, rows, length), jnp.bfloat16)
    return pl.pallas_call(
        functools.partial(share_kernel, size),
        in_specs=[pl.BlockSpec(memory_space=pltpu.VMEM)],
        out_specs=pl.BlockSpec(memory_space=pltpu.VMEM),
        out_shape=jax.ShapeDtypeStruct((rows, samples), jnp.bfloat16),
        scratch_shapes=[
            blocks(size),
            blocks(size),
            blocks(size),
            pltpu.SemaphoreType.DMA((2 * stages,)),
            pltpu.SemaphoreType.DMA((2 * stages,)),
        ],
        compiler_params=pltpu.CompilerParams(
            collective_id=0, has_side_effects=True, vmem_limit_bytes=VMEM
        ),
        name="share",
    )(mine)


def neighbours(live, traces):
    count = lax.axis_size("fiber")
    up = [(i, i + 1) for i in range(count - 1)]
    down = [(i + 1, i) for i in range(count - 1)]
    mask = live.astype(jnp.bfloat16)[:, None]
    low = lax.ppermute(traces[-RIM:] * mask[-RIM:], "fiber", up)
    high = lax.ppermute(traces[:RIM] * mask[:RIM], "fiber", down)
    return low, high


def filter_weights(live, source_channels, source_owner):
    channels = live.shape[0]
    alive = live.astype(jnp.float32)
    column = jnp.concatenate([alive, jnp.ones((2 * RIM,), jnp.float32)])
    weight = tap_matrix(channels) * alive[:, None] * column[None, :]
    mine = (source_owner == lax.axis_index("fiber"))[:, None]
    chosen = jnp.where(mine, source_channels, -1).reshape(-1)
    pick = chosen[:, None] == jnp.arange(channels)[None, :]
    picked = jnp.sum(jnp.where(pick[:, :, None], weight[None], 0.0), axis=1)
    return jnp.concatenate([weight, picked], axis=0).astype(jnp.bfloat16)


def on_device(traces, live_mask, source_channels, source_owner):
    steps, per_step = source_channels.shape
    low, high = neighbours(live_mask, traces)
    weight = filter_weights(live_mask, source_channels, source_owner)
    filtered, mine = spatial_filter(weight, traces, low, high)
    arrived = share(mine)
    whitened = whiten(filtered, 8)
    sources = whiten(arrived, 16)
    out = cross(sources, whitened)
    return out.reshape(steps, per_step, live_mask.shape[0], FRAME)


def solution(mesh):
    placed = (P(("group", "fiber"), None), P(("group", "fiber")), P("group", None), P("group"))
    return jax.shard_map(
        on_device,
        mesh=mesh,
        in_specs=placed,
        out_specs=P(None, None, ("group", "fiber"), None),
        check_vma=False,
    )
```

```python
import functools

import jax
import jax.numpy as jnp
import numpy as np
from jax import lax
from jax.experimental import pallas as pl
from jax.experimental.pallas import tpu as pltpu
from jax.sharding import PartitionSpec as P

FRAME = 2048
HOP = FRAME // 2
BINS = FRAME // 2
SMOOTH = 64
RIM = 8
LANES = 128
VMEM = 56 * 1024 * 1024


def dft_table():
    n = np.arange(FRAME)
    k = np.arange(BINS)
    phase = 2.0 * np.pi / FRAME * (n[:, None] * k[None, :] % FRAME)
    hann = 0.5 - 0.5 * np.cos(2.0 * np.pi / FRAME * n)
    table = np.concatenate(
        [hann[:, None] * np.cos(phase), -hann[:, None] * np.sin(phase)], axis=1
    )
    return table.astype(np.float32).astype(jnp.bfloat16)


def band_matrix():
    k = np.arange(BINS)
    inside = np.abs(k[:, None] - k[None, :]) <= SMOOTH
    recip = (1.0 / inside.sum(axis=0)).astype(np.float32)
    return inside.astype(np.float32).astype(jnp.bfloat16), recip[None, :]


def tap_matrix(channels):
    place = np.concatenate(
        [np.arange(channels), np.arange(-RIM, 0), np.arange(channels, channels + RIM)]
    )
    distance = np.abs(np.arange(channels)[:, None] - place[None, :])
    taps = np.where(distance <= RIM, -(RIM + 1.0 - distance), 0.0)
    return np.where(distance == 0, RIM * (RIM + 1.0), taps).astype(np.float32)


def filter_kernel(channels, weight_ref, own_ref, low_ref, high_ref, out_ref, src_ref):
    rows = jnp.concatenate([own_ref[...], low_ref[...], high_ref[...]], axis=0)
    total = jnp.dot(weight_ref[...], rows, preferred_element_type=jnp.float32)
    total = (total * (1.0 / (RIM * (RIM + 1.0)))).astype(jnp.bfloat16)
    out_ref[...] = total[:channels]
    src_ref[...] = total[channels:]


def spatial_filter(weight, own, low, high):
    channels, samples = own.shape
    sources = weight.shape[0] - channels
    blocks = samples // HOP
    chunk = HOP * (7 if blocks % 7 == 0 else 1)
    columns = lambda rows: pl.BlockSpec((rows, chunk), lambda i: (0, i))
    return pl.pallas_call(
        functools.partial(filter_kernel, channels),
        grid=(samples // chunk,),
        in_specs=[
            pl.BlockSpec(weight.shape, lambda i: (0, 0)),
            columns(channels),
            columns(RIM),
            columns(RIM),
        ],
        out_specs=[columns(channels), columns(sources)],
        out_shape=[
            jax.ShapeDtypeStruct((channels, samples), jnp.bfloat16),
            jax.ShapeDtypeStruct((sources, samples), jnp.bfloat16),
        ],
        compiler_params=pltpu.CompilerParams(vmem_limit_bytes=VMEM),
        name="spatial_filter",
    )(weight, own, low, high)


def whiten_frames(x_ref, first, count, tables, out_ref, spec_ref, pow_ref, between=None):
    table_ref, band_ref, recip_ref = tables
    rows = x_ref.shape[0]
    frames = jnp.concatenate(
        [
            x_ref[:, pl.ds(pl.multiple_of((first + i) * HOP, HOP), FRAME)]
            for i in range(count)
        ],
        axis=0,
    )
    used = slice(0, count * rows)
    width = 256
    for lo in range(0, BINS, width):
        if between is not None and lo == BINS // 2:
            between()
        real = jnp.dot(
            frames, table_ref[:, lo : lo + width], preferred_element_type=jnp.float32
        )
        imag = jnp.dot(
            frames,
            table_ref[:, BINS + lo : BINS + lo + width],
            preferred_element_type=jnp.float32,
        )
        spec_ref[used, lo : lo + width] = real
        spec_ref[used, BINS + lo : BINS + lo + width] = imag
        pow_ref[used, lo : lo + width] = (real * real + imag * imag).astype(jnp.bfloat16)
    for lo in range(0, BINS, width):
        start, stop = max(0, lo - LANES), min(BINS, lo + width + LANES)
        smooth = jnp.dot(
            pow_ref[used, start:stop],
            band_ref[start:stop, lo : lo + width],
            preferred_element_type=jnp.float32,
        )
        factor = lax.rsqrt(smooth * recip_ref[:, lo : lo + width] + 1e-06)
        for at in (lo, BINS + lo):
            white = (spec_ref[used, at : at + width] * factor).astype(jnp.bfloat16)
            for i in range(count):
                out_ref[i, :, at : at + width] = white[i * rows : (i + 1) * rows]


def share_stages(size):
    return [1 << i for i in range(size.bit_length() - 1)]


def share_actions(size, x_ref, arrived, held, landed, result, send_sem, recv_sem):
    me = lax.axis_index("fiber")
    stages = share_stages(size)
    samples = x_ref.shape[1]
    length = held.shape[2]
    sides = [lax.rem(me // bit, 2) for bit in stages]
    partners = [me + bit - 2 * bit * side for bit, side in zip(stages, sides)]

    def remote(i, source, target, phase):
        return pltpu.make_async_remote_copy(
            src_ref=source,
            dst_ref=target,
            send_sem=send_sem.at[phase],
            recv_sem=recv_sem.at[phase],
            device_id={"fiber": partners[i]},
            device_id_type=pl.DeviceIdType.MESH,
        )

    first, count, at = 0, size, 0
    copies, ends, spans = [], [], []

    def adding(kept, count, at):
        def run():
            for j in range(count):
                held[kept + j] = held[kept + j] + landed[at + j]

        return run

    for i, side in enumerate(sides):
        spans.append(first)
        count //= 2
        kept = first + side * count
        sent = first + (1 - side) * count
        copies.append(
            remote(i, held.at[pl.ds(sent, count)], landed.at[pl.ds(at, count)], i)
        )
        ends.append(adding(kept, count, at))
        at += count
        first = kept

    last = first

    def keep():
        result[last] = held[last]

    for i in reversed(range(len(stages))):
        part = result.at[pl.ds(first, count)]
        copies.append(remote(i, part, part, len(stages) + i))
        ends.append(None)
        first = spans[i]
        count *= 2

    def enter():
        barrier = pltpu.get_barrier_semaphore()
        for partner in partners:
            pl.semaphore_signal(
                barrier,
                inc=1,
                device_id={"fiber": partner},
                device_id_type=pl.DeviceIdType.MESH,
            )
        for j in range(size):
            stop = min(samples, (j + 1) * length)
            if stop < (j + 1) * length:
                held[j] = jnp.zeros(held.shape[1:], held.dtype)
            if stop > j * length:
                held[j, :, : stop - j * length] = x_ref[:, j * length : stop]
        pl.semaphore_wait(barrier, len(stages))
        copies[0].start()

    def middle(phase):
        def run():
            copies[phase - 1].wait()
            if ends[phase - 1] is not None:
                ends[phase - 1]()
            if phase == len(stages):
                keep()
            copies[phase].start()

        return run

    def leave():
        copies[-1].wait()
        for j in range(size):
            stop = min(samples, (j + 1) * length)
            if stop > j * length:
                arrived[:, j * length : stop] = result[j, :, : stop - j * length]

    return [enter] + [middle(phase) for phase in range(1, len(copies))] + [leave]


def whiten_kernel(
    size, own_count, src_count, own_steps,
    x_ref, mine_ref, table_ref, band_ref, recip_ref,
    own_ref, src_ref,
    spec_ref, pow_ref, arrived, held, landed, result, send_sem, recv_sem,
):
    step = pl.program_id(0)
    tables = (table_ref, band_ref, recip_ref)
    actions = share_actions(
        size, mine_ref, arrived, held, landed, result, send_sem, recv_sem
    )
    slots = 2 * own_steps
    moves = len(actions) - 1
    when = [q * slots // moves for q in range(moves)]

    def progress(half):
        for q, slot in enumerate(when):
            if slot % 2 == half:
                pl.when(step == slot // 2)(actions[q])

    @pl.when(step < own_steps)
    def _():
        progress(0)
        whiten_frames(
            x_ref, step * own_count, own_count, tables, own_ref, spec_ref, pow_ref,
            lambda: progress(1),
        )

    pl.when(step == own_steps)(actions[-1])

    @pl.when(step >= own_steps)
    def _():
        whiten_frames(
            arrived, (step - own_steps) * src_count, src_count, tables, src_ref,
            spec_ref, pow_ref,
        )


def whiten(filtered, mine, own_count, src_count):
    rows, samples = filtered.shape
    sources = mine.shape[0]
    frames = samples // HOP - 1
    size = lax.axis_size("fiber")
    length = -(-samples // (size * LANES)) * LANES
    phases = 2 * len(share_stages(size))
    own_steps, src_steps = frames // own_count, frames // src_count
    band, recip = band_matrix()
    whole = lambda shape: pl.BlockSpec(
        shape, lambda i: (0,) * len(shape), pipeline_mode=pl.Buffered(1)
    )
    blocks = pltpu.VMEM((size, sources, length), jnp.bfloat16)
    depth = max(own_count * rows, src_count * sources)
    return pl.pallas_call(
        functools.partial(whiten_kernel, size, own_count, src_count, own_steps),
        grid=(own_steps + src_steps,),
        in_specs=[
            whole((rows, samples)),
            whole((sources, samples)),
            whole((FRAME, FRAME)),
            whole((BINS, BINS)),
            whole((1, BINS)),
        ],
        out_specs=[
            pl.BlockSpec(
                (own_count, rows, FRAME),
                lambda i: (i - (i // own_steps) * (i - own_steps + 1), 0, 0),
            ),
            pl.BlockSpec(
                (src_count, sources, FRAME),
                lambda i: ((i // own_steps) * (i - own_steps), 0, 0),
            ),
        ],
        out_shape=[
            jax.ShapeDtypeStruct((frames, rows, FRAME), jnp.bfloat16),
            jax.ShapeDtypeStruct((frames, sources, FRAME), jnp.bfloat16),
        ],
        scratch_shapes=[
            pltpu.VMEM((depth, FRAME), jnp.float32),
            pltpu.VMEM((depth, BINS), jnp.bfloat16),
            pltpu.VMEM((sources, samples), jnp.bfloat16),
            blocks,
            blocks,
            blocks,
            pltpu.SemaphoreType.DMA((phases,)),
            pltpu.SemaphoreType.DMA((phases,)),
        ],
        compiler_params=pltpu.CompilerParams(
            collective_id=0, has_side_effects=True, vmem_limit_bytes=VMEM
        ),
        cost_estimate=pl.CostEstimate(
            flops=2 * frames * (rows + sources) * FRAME * FRAME,
            bytes_accessed=8 * FRAME * FRAME,
            transcendentals=frames * (rows + sources) * BINS,
        ),
        name="whiten",
    )(filtered, mine, dft_table(), band, recip)


def cross_kernel(sr_ref, si_ref, wr_ref, wi_ref, out_ref, c_ref, d_ref, e_ref, a_ref, p_ref, m_ref):
    frames, sources, _ = sr_ref.shape
    channels = wr_ref.shape[1]
    at = pl.multiple_of(pl.program_id(0) * LANES, LANES)

    @pl.loop(0, frames)
    def _(f):
        c = wr_ref[f].astype(jnp.float32)
        d = wi_ref[f].astype(jnp.float32)
        c_ref[f] = c
        d_ref[f] = d
        e_ref[f] = c + d
        a = sr_ref[f].astype(jnp.float32) * (1.0 / frames)
        b = si_ref[f].astype(jnp.float32) * (1.0 / frames)
        a_ref[f] = a
        p_ref[f] = a + b
        m_ref[f] = b - a

    pieces = channels // 8
    together = 2
    for s in range(0, sources, together):

        def step(f, sums):
            sums = list(sums)
            taps = []
            for t in range(together):
                row = pl.ds(s + t, 1)
                taps.append(
                    tuple(
                        jnp.broadcast_to(ref[f, row, :], (8, LANES))
                        for ref in (a_ref, p_ref, m_ref)
                    )
                )
            for v in range(pieces):
                part = slice(8 * v, 8 * v + 8)
                c, d, e = c_ref[f, part, :], d_ref[f, part, :], e_ref[f, part, :]
                for t in range(together):
                    a, p, m = taps[t]
                    base = 3 * (t * pieces + v)
                    sums[base] = sums[base] + a * e
                    sums[base + 1] = sums[base + 1] + p * c
                    sums[base + 2] = sums[base + 2] + m * d
            return tuple(sums)

        zero = jnp.zeros((8, LANES), jnp.float32)
        sums = lax.fori_loop(0, frames, step, (zero,) * (3 * together * pieces), unroll=4)
        for t in range(together):
            for v in range(pieces):
                base = 3 * (t * pieces + v)
                part = slice(8 * v, 8 * v + 8)
                out_ref[s + t, part, pl.ds(at, LANES)] = sums[base] + sums[base + 2]
                out_ref[s + t, part, pl.ds(BINS + at, LANES)] = sums[base] - sums[base + 1]


def cross(sources, whitened):
    frames, channels, _ = whitened.shape
    count = sources.shape[1]
    tiles = BINS // LANES
    real = lambda rows: pl.BlockSpec((frames, rows, LANES), lambda j: (0, 0, j))
    imag = lambda rows: pl.BlockSpec((frames, rows, LANES), lambda j: (0, 0, tiles + j))
    tile = lambda rows: pltpu.VMEM((frames, rows, LANES), jnp.float32)
    return pl.pallas_call(
        cross_kernel,
        grid=(tiles,),
        in_specs=[real(count), imag(count), real(channels), imag(channels)],
        out_specs=pl.BlockSpec(
            (count, channels, FRAME), lambda j: (0, 0, 0), pipeline_mode=pl.Buffered(1)
        ),
        out_shape=jax.ShapeDtypeStruct((count, channels, FRAME), jnp.float32),
        scratch_shapes=[tile(channels)] * 3 + [tile(count)] * 3,
        compiler_params=pltpu.CompilerParams(vmem_limit_bytes=VMEM),
        name="cross",
    )(sources, sources, whitened, whitened)


def neighbours(live, traces):
    count = lax.axis_size("fiber")
    up = [(i, i + 1) for i in range(count - 1)]
    down = [(i + 1, i) for i in range(count - 1)]
    mask = live.astype(jnp.bfloat16)[:, None]
    low = lax.ppermute(traces[-RIM:] * mask[-RIM:], "fiber", up)
    high = lax.ppermute(traces[:RIM] * mask[:RIM], "fiber", down)
    return low, high


def filter_weights(live, source_channels, source_owner):
    channels = live.shape[0]
    alive = live.astype(jnp.float32)
    column = jnp.concatenate([alive, jnp.ones((2 * RIM,), jnp.float32)])
    weight = tap_matrix(channels) * alive[:, None] * column[None, :]
    mine = (source_owner == lax.axis_index("fiber"))[:, None]
    chosen = jnp.where(mine, source_channels, -1).reshape(-1)
    pick = chosen[:, None] == jnp.arange(channels)[None, :]
    picked = jnp.sum(jnp.where(pick[:, :, None], weight[None], 0.0), axis=1)
    return jnp.concatenate([weight, picked], axis=0).astype(jnp.bfloat16)


def on_device(traces, live_mask, source_channels, source_owner):
    steps, per_step = source_channels.shape
    low, high = neighbours(live_mask, traces)
    weight = filter_weights(live_mask, source_channels, source_owner)
    filtered, mine = spatial_filter(weight, traces, low, high)
    whitened, sources = whiten(filtered, mine, 8, 24)
    out = cross(sources, whitened)
    return out.reshape(steps, per_step, live_mask.shape[0], FRAME)


def solution(mesh):
    placed = (P(("group", "fiber"), None), P(("group", "fiber")), P("group", None), P("group"))
    return jax.shard_map(
        on_device,
        mesh=mesh,
        in_specs=placed,
        out_specs=P(None, None, ("group", "fiber"), None),
        check_vma=False,
    )
```

```python
import functools

import jax
import jax.numpy as jnp
import numpy as np
from jax import lax
from jax.experimental import pallas as pl
from jax.experimental.pallas import tpu as pltpu
from jax.sharding import PartitionSpec as P

FRAME = 2048
HOP = FRAME // 2
BINS = FRAME // 2
SMOOTH = 64
RIM = 8
LANES = 128
VMEM = 56 * 1024 * 1024


def dft_table():
    n = np.arange(FRAME)
    k = np.arange(BINS)
    phase = 2.0 * np.pi / FRAME * (n[:, None] * k[None, :] % FRAME)
    hann = 0.5 - 0.5 * np.cos(2.0 * np.pi / FRAME * n)
    table = np.concatenate(
        [hann[:, None] * np.cos(phase), -hann[:, None] * np.sin(phase)], axis=1
    )
    return table.astype(np.float32).astype(jnp.bfloat16)


def band_matrix():
    k = np.arange(BINS)
    inside = np.abs(k[:, None] - k[None, :]) <= SMOOTH
    recip = (1.0 / inside.sum(axis=0)).astype(np.float32)
    return inside.astype(np.float32).astype(jnp.bfloat16), recip[None, :]


def tap_matrix(channels):
    place = np.concatenate(
        [np.arange(channels), np.arange(-RIM, 0), np.arange(channels, channels + RIM)]
    )
    distance = np.abs(np.arange(channels)[:, None] - place[None, :])
    taps = np.where(distance <= RIM, -(RIM + 1.0 - distance), 0.0)
    return np.where(distance == 0, RIM * (RIM + 1.0), taps).astype(np.float32)


def filter_kernel(channels, weight_ref, own_ref, low_ref, high_ref, out_ref, src_ref):
    rows = jnp.concatenate([own_ref[...], low_ref[...], high_ref[...]], axis=0)
    total = jnp.dot(weight_ref[...], rows, preferred_element_type=jnp.float32)
    total = (total * (1.0 / (RIM * (RIM + 1.0)))).astype(jnp.bfloat16)
    out_ref[...] = total[:channels]
    src_ref[...] = total[channels:]


def spatial_filter(weight, own, low, high):
    channels, samples = own.shape
    sources = weight.shape[0] - channels
    blocks = samples // HOP
    chunk = HOP * (7 if blocks % 7 == 0 else 1)
    columns = lambda rows: pl.BlockSpec((rows, chunk), lambda i: (0, i))
    return pl.pallas_call(
        functools.partial(filter_kernel, channels),
        grid=(samples // chunk,),
        in_specs=[
            pl.BlockSpec(weight.shape, lambda i: (0, 0)),
            columns(channels),
            columns(RIM),
            columns(RIM),
        ],
        out_specs=[columns(channels), columns(sources)],
        out_shape=[
            jax.ShapeDtypeStruct((channels, samples), jnp.bfloat16),
            jax.ShapeDtypeStruct((sources, samples), jnp.bfloat16),
        ],
        compiler_params=pltpu.CompilerParams(vmem_limit_bytes=VMEM),
        name="spatial_filter",
    )(weight, own, low, high)


def whiten_frames(x_ref, first, count, tables, out_ref, spec_ref, pow_ref, between=None):
    table_ref, band_ref, recip_ref = tables
    rows = x_ref.shape[0]
    frames = jnp.concatenate(
        [
            x_ref[:, pl.ds(pl.multiple_of((first + i) * HOP, HOP), FRAME)]
            for i in range(count)
        ],
        axis=0,
    )
    used = slice(0, count * rows)
    width = 256
    for lo in range(0, BINS, width):
        if between is not None and lo == BINS // 2:
            between()
        real = jnp.dot(
            frames, table_ref[:, lo : lo + width], preferred_element_type=jnp.float32
        )
        imag = jnp.dot(
            frames,
            table_ref[:, BINS + lo : BINS + lo + width],
            preferred_element_type=jnp.float32,
        )
        spec_ref[used, lo : lo + width] = real
        spec_ref[used, BINS + lo : BINS + lo + width] = imag
        pow_ref[used, lo : lo + width] = (real * real + imag * imag).astype(jnp.bfloat16)
    for lo in range(0, BINS, width):
        start, stop = max(0, lo - LANES), min(BINS, lo + width + LANES)
        smooth = jnp.dot(
            pow_ref[used, start:stop],
            band_ref[start:stop, lo : lo + width],
            preferred_element_type=jnp.float32,
        )
        factor = lax.rsqrt(smooth * recip_ref[:, lo : lo + width] + 1e-06)
        for at in (lo, BINS + lo):
            white = (spec_ref[used, at : at + width] * factor).astype(jnp.bfloat16)
            for i in range(count):
                out_ref[i, :, at : at + width] = white[i * rows : (i + 1) * rows]


def share_stages(size):
    return [1 << i for i in range(size.bit_length() - 1)]


def share_actions(
    size, stages, base, samples, greet,
    x_ref, arrived, held, landed, result, send_sem, recv_sem,
):
    me = lax.axis_index("fiber")
    length = held.shape[2]
    sides = [lax.rem(me // bit, 2) for bit in stages]
    partners = [me + bit - 2 * bit * side for bit, side in zip(stages, sides)]

    def remote(i, source, target, phase):
        return pltpu.make_async_remote_copy(
            src_ref=source,
            dst_ref=target,
            send_sem=send_sem.at[phase],
            recv_sem=recv_sem.at[phase],
            device_id={"fiber": partners[i]},
            device_id_type=pl.DeviceIdType.MESH,
        )

    first, count, at = 0, size, 0
    copies, ends, spans = [], [], []

    def adding(kept, count, at):
        def run():
            for j in range(count):
                held[kept + j] = held[kept + j] + landed[at + j]

        return run

    for i, side in enumerate(sides):
        spans.append(first)
        count //= 2
        kept = first + side * count
        sent = first + (1 - side) * count
        copies.append(
            remote(i, held.at[pl.ds(sent, count)], landed.at[pl.ds(at, count)], i)
        )
        ends.append(adding(kept, count, at))
        at += count
        first = kept

    last = first

    def keep():
        result[last] = held[last]

    for i in reversed(range(len(stages))):
        part = result.at[pl.ds(first, count)]
        copies.append(remote(i, part, part, len(stages) + i))
        ends.append(None)
        first = spans[i]
        count *= 2

    def enter():
        if greet:
            barrier = pltpu.get_barrier_semaphore()
            for partner in partners:
                pl.semaphore_signal(
                    barrier,
                    inc=1,
                    device_id={"fiber": partner},
                    device_id_type=pl.DeviceIdType.MESH,
                )
            pl.semaphore_wait(barrier, len(stages))
        for j in range(size):
            stop = min(samples, (j + 1) * length)
            if stop < (j + 1) * length:
                held[j] = jnp.zeros(held.shape[1:], held.dtype)
            if stop > j * length:
                held[j, :, : stop - j * length] = x_ref[:, base + j * length : base + stop]
        copies[0].start()

    def middle(phase):
        def run():
            copies[phase - 1].wait()
            if ends[phase - 1] is not None:
                ends[phase - 1]()
            if phase == len(stages):
                keep()
            copies[phase].start()

        return run

    def leave():
        copies[-1].wait()
        for j in range(size):
            stop = min(samples, (j + 1) * length)
            if stop > j * length:
                arrived[:, base + j * length : base + stop] = result[j, :, : stop - j * length]

    return [enter] + [middle(phase) for phase in range(1, len(copies))] + [leave]


def whiten_kernel(
    size, own_count, src_count, own_steps,
    x_ref, mine_ref, table_ref, band_ref, recip_ref,
    own_ref, src_ref,
    spec_ref, pow_ref, arrived, *ways,
):
    step = pl.program_id(0)
    tables = (table_ref, band_ref, recip_ref)
    half = mine_ref.shape[1] // 2
    near = share_stages(size)
    far = near[:1] + near[2:] + near[1:2]
    one = share_actions(size, near, 0, half, True, mine_ref, arrived, *ways[:5])
    two = share_actions(size, far, half, half, False, mine_ref, arrived, *ways[5:])

    def both(first, second):
        def run():
            first()
            second()

        return run

    actions = [both(first, second) for first, second in zip(one, two)]
    slots = 2 * own_steps
    moves = len(actions) - 1
    when = [q * slots // moves for q in range(moves)]

    def progress(half):
        for q, slot in enumerate(when):
            if slot % 2 == half:
                pl.when(step == slot // 2)(actions[q])

    @pl.when(step < own_steps)
    def _():
        progress(0)
        whiten_frames(
            x_ref, step * own_count, own_count, tables, own_ref, spec_ref, pow_ref,
            lambda: progress(1),
        )

    pl.when(step == own_steps)(actions[-1])

    @pl.when(step >= own_steps)
    def _():
        whiten_frames(
            arrived, (step - own_steps) * src_count, src_count, tables, src_ref,
            spec_ref, pow_ref,
        )


def whiten(filtered, mine, own_count, src_count):
    rows, samples = filtered.shape
    sources = mine.shape[0]
    frames = samples // HOP - 1
    size = lax.axis_size("fiber")
    length = -(-samples // (2 * size * LANES)) * LANES
    phases = 2 * len(share_stages(size))
    own_steps, src_steps = frames // own_count, frames // src_count
    band, recip = band_matrix()
    whole = lambda shape: pl.BlockSpec(
        shape, lambda i: (0,) * len(shape), pipeline_mode=pl.Buffered(1)
    )
    blocks = pltpu.VMEM((size, sources, length), jnp.bfloat16)
    way = [blocks] * 3 + [pltpu.SemaphoreType.DMA((phases,))] * 2
    depth = max(own_count * rows, src_count * sources)
    return pl.pallas_call(
        functools.partial(whiten_kernel, size, own_count, src_count, own_steps),
        grid=(own_steps + src_steps,),
        in_specs=[
            whole((rows, samples)),
            whole((sources, samples)),
            whole((FRAME, FRAME)),
            whole((BINS, BINS)),
            whole((1, BINS)),
        ],
        out_specs=[
            pl.BlockSpec(
                (own_count, rows, FRAME),
                lambda i: (i - (i // own_steps) * (i - own_steps + 1), 0, 0),
            ),
            pl.BlockSpec(
                (src_count, sources, FRAME),
                lambda i: ((i // own_steps) * (i - own_steps), 0, 0),
            ),
        ],
        out_shape=[
            jax.ShapeDtypeStruct((frames, rows, FRAME), jnp.bfloat16),
            jax.ShapeDtypeStruct((frames, sources, FRAME), jnp.bfloat16),
        ],
        scratch_shapes=[
            pltpu.VMEM((depth, FRAME), jnp.float32),
            pltpu.VMEM((depth, BINS), jnp.bfloat16),
            pltpu.VMEM((sources, samples), jnp.bfloat16),
            *way,
            *way,
        ],
        compiler_params=pltpu.CompilerParams(
            collective_id=0, has_side_effects=True, vmem_limit_bytes=VMEM
        ),
        cost_estimate=pl.CostEstimate(
            flops=2 * frames * (rows + sources) * FRAME * FRAME,
            bytes_accessed=8 * FRAME * FRAME,
            transcendentals=frames * (rows + sources) * BINS,
        ),
        name="whiten",
    )(filtered, mine, dft_table(), band, recip)


def cross_kernel(sr_ref, si_ref, wr_ref, wi_ref, out_ref, c_ref, d_ref, a_ref, p_ref, m_ref):
    frames, sources, _ = sr_ref.shape
    channels = wr_ref.shape[1]
    at = pl.multiple_of(pl.program_id(0) * LANES, LANES)

    @pl.loop(0, frames)
    def _(f):
        c_ref[f] = wr_ref[f].astype(jnp.float32)
        d_ref[f] = wi_ref[f].astype(jnp.float32)
        a = sr_ref[f].astype(jnp.float32) * (1.0 / frames)
        b = si_ref[f].astype(jnp.float32) * (1.0 / frames)
        a_ref[f] = a
        p_ref[f] = a + b
        m_ref[f] = b - a

    pieces = channels // 8
    group = 3 if pieces % 3 == 0 else 1
    together = 4
    for s in range(0, sources, together):
        for start in range(0, pieces, group):

            def step(f, sums):
                sums = list(sums)
                parts = []
                for v in range(group):
                    part = slice(8 * (start + v), 8 * (start + v) + 8)
                    c, d = c_ref[f, part, :], d_ref[f, part, :]
                    parts.append((c + d, c, d))
                for t in range(together):
                    row = pl.ds(s + t, 1)
                    taps = [
                        jnp.broadcast_to(ref[f, row, :], (8, LANES))
                        for ref in (a_ref, p_ref, m_ref)
                    ]
                    for v in range(group):
                        for u in range(3):
                            base = 3 * (t * group + v) + u
                            sums[base] = sums[base] + taps[u] * parts[v][u]
                return tuple(sums)

            zero = jnp.zeros((8, LANES), jnp.float32)
            sums = lax.fori_loop(0, frames, step, (zero,) * (3 * together * group), unroll=4)
            for t in range(together):
                for v in range(group):
                    one, two, three = sums[3 * (t * group + v) : 3 * (t * group + v) + 3]
                    part = slice(8 * (start + v), 8 * (start + v) + 8)
                    out_ref[s + t, part, pl.ds(at, LANES)] = one + three
                    out_ref[s + t, part, pl.ds(BINS + at, LANES)] = one - two


def cross(sources, whitened):
    frames, channels, _ = whitened.shape
    count = sources.shape[1]
    tiles = BINS // LANES
    real = lambda rows: pl.BlockSpec((frames, rows, LANES), lambda j: (0, 0, j))
    imag = lambda rows: pl.BlockSpec((frames, rows, LANES), lambda j: (0, 0, tiles + j))
    tile = lambda rows: pltpu.VMEM((frames, rows, LANES), jnp.float32)
    return pl.pallas_call(
        cross_kernel,
        grid=(tiles,),
        in_specs=[real(count), imag(count), real(channels), imag(channels)],
        out_specs=pl.BlockSpec(
            (count, channels, FRAME), lambda j: (0, 0, 0), pipeline_mode=pl.Buffered(1)
        ),
        out_shape=jax.ShapeDtypeStruct((count, channels, FRAME), jnp.float32),
        scratch_shapes=[tile(channels)] * 2 + [tile(count)] * 3,
        compiler_params=pltpu.CompilerParams(vmem_limit_bytes=VMEM),
        name="cross",
    )(sources, sources, whitened, whitened)


def neighbours(live, traces):
    count = lax.axis_size("fiber")
    up = [(i, i + 1) for i in range(count - 1)]
    down = [(i + 1, i) for i in range(count - 1)]
    mask = live.astype(jnp.bfloat16)[:, None]
    low = lax.ppermute(traces[-RIM:] * mask[-RIM:], "fiber", up)
    high = lax.ppermute(traces[:RIM] * mask[:RIM], "fiber", down)
    return low, high


def filter_weights(live, source_channels, source_owner):
    channels = live.shape[0]
    alive = live.astype(jnp.float32)
    column = jnp.concatenate([alive, jnp.ones((2 * RIM,), jnp.float32)])
    weight = tap_matrix(channels) * alive[:, None] * column[None, :]
    mine = (source_owner == lax.axis_index("fiber"))[:, None]
    chosen = jnp.where(mine, source_channels, -1).reshape(-1)
    pick = chosen[:, None] == jnp.arange(channels)[None, :]
    picked = jnp.sum(jnp.where(pick[:, :, None], weight[None], 0.0), axis=1)
    return jnp.concatenate([weight, picked], axis=0).astype(jnp.bfloat16)


def on_device(traces, live_mask, source_channels, source_owner):
    steps, per_step = source_channels.shape
    low, high = neighbours(live_mask, traces)
    weight = filter_weights(live_mask, source_channels, source_owner)
    filtered, mine = spatial_filter(weight, traces, low, high)
    whitened, sources = whiten(filtered, mine, 8, 24)
    out = cross(sources, whitened)
    return out.reshape(steps, per_step, live_mask.shape[0], FRAME)


def solution(mesh):
    placed = (P(("group", "fiber"), None), P(("group", "fiber")), P("group", None), P("group"))
    return jax.shard_map(
        on_device,
        mesh=mesh,
        in_specs=placed,
        out_specs=P(None, None, ("group", "fiber"), None),
        check_vma=False,
    )
```
